32 devices in a mesh: groups: 2 (over x), tensor: 16 (over z, y, core).
Axes of the slice: x: 2, y: 2, z: 4, core: 2. Of those that a mesh axis runs over, the one named last changes fastest.
Arguments:
- residual: bfloat16 [64, 8192], P(('groups', 'tensor')), parts along dimension 0, may hold values from -6 to 6
- context: bfloat16 [64, 2048], P('groups', 'tensor'), parts along dimension 0, may hold values from -6 to 6
- w_out: bfloat16 [2048, 8192], P('tensor'), may hold values from -0.125 to 0.125
- ffn_gain: bfloat16 [8192], replicated, may hold values from 0.099609375 to 1.8984375
- w_gate: bfloat16 [8192, 3584], P(None, 'tensor'), may hold values from -0.0625 to 0.0625
- w_up: bfloat16 [8192, 3584], P(None, 'tensor'), may hold values from -0.0625 to 0.0625
- w_down: bfloat16 [3584, 8192], P('tensor'), may hold values from -0.09375 to 0.09375
Outputs:
- layer_out: bfloat16 [64, 8192], P(('groups', 'tensor')), parts along dimension 0
The draws below stay inside these ranges and needn't reach their ends.
There are 2 independent parts, one for each index of `groups`. The reference program is written for one: setup_inputs(seed, part) draws one part's arguments, and reference() takes and returns one part's arrays. A program takes and returns all parts, laid end to end along the dimension named above; an argument that names none is the same for every part. Nothing has to cross between parts.
All inputs are finite; a program needn't handle non-finite values. Where the reference program divides by a largest or mean magnitude, that divisor is 1e-20 or more.
Results may differ from the reference program's by a relative error of at most 0.018.
Values may be sent and summed in bfloat16 or wider, within the bound.
A program may use at most 128 MiB of HBM per device.

```python
import math
import jax
import jax.numpy as jnp
from jax import lax

D = 8192
HD = 128
BLOCK = 128
FF_DEV = 224
HEADS = 16
FF = 3584
ROWS = 32
N_TENSOR = 16


def levels(rng, shape, shards, low, high):
    level = 1.0
    for dim, parts in shards:
        steps = jax.random.uniform(jax.random.fold_in(jax.random.fold_in(rng, 6), dim), (parts,), jnp.float32, low / len(shards), high / len(shards))
        level = level * jnp.repeat(jnp.exp(steps), shape[dim] // parts).reshape((-1,) + (1,) * (len(shape) - 1 - dim))
    return level


def gaussian(rng, dims, width, reach, shards=(), dtype=jnp.bfloat16):
    result = width * jax.random.normal(rng, dims, jnp.float32)
    if shards:
        result = result * levels(rng, dims, shards, -0.22, 0.18)
    return jnp.clip(result, -reach, reach).astype(dtype)


def setup_inputs(seed: int = 0, part: int = 0) -> dict:
    keys = jax.random.split(jax.random.key(seed), 8)
    own_keys = jax.random.split(jax.random.fold_in(keys[7], part), 8)
    residual = gaussian(own_keys[0], (ROWS, D), 1.0, 6.0, ((0, 16),))
    context = gaussian(own_keys[1], (ROWS, HEADS * HD), 1.0, 6.0, ((1, 16),))
    w_out = gaussian(keys[2], (HEADS * HD, D), (HEADS * HD) ** -0.5, 0.125, ((0, 16),))
    ffn_gain = jnp.clip(1.0 + 0.18 * jax.random.normal(keys[3], (D,), jnp.float32), 0.099609375, 1.8984375).astype(jnp.bfloat16)
    w_gate = gaussian(keys[4], (D, FF), D ** -0.5, 0.0625, ((1, 16),))
    w_up = gaussian(keys[5], (D, FF), D ** -0.5, 0.0625, ((1, 16),))
    w_down = gaussian(keys[6], (FF, D), FF ** -0.5, 0.09375, ((0, 16),))
    return {"residual": residual, "context": context, "w_out": w_out, "ffn_gain": ffn_gain, "w_gate": w_gate, "w_up": w_up, "w_down": w_down}


CLIP_LEVEL = 3.0
SCALE_EPS = 1e-06
NORM_EPS = 1e-05

def sylvester(block_order):
    hadamard = jnp.ones((1, 1), jnp.float32)
    while hadamard.shape[0] < block_order:
        upper = jnp.concatenate([hadamard, hadamard], axis=1)
        lower = jnp.concatenate([hadamard, -hadamard], axis=1)
        hadamard = jnp.concatenate([upper, lower], axis=0)
    return hadamard

def rotate(values):
    row_count = values.shape[0]
    hadamard = jnp.asarray(sylvester(BLOCK), jnp.bfloat16)
    flat = values.reshape(-1, BLOCK)
    high_part = flat.astype(jnp.bfloat16)
    low_part = (flat - high_part.astype(jnp.float32)).astype(jnp.bfloat16)
    turned = jnp.dot(high_part, hadamard, preferred_element_type=jnp.float32)
    turned = turned + jnp.dot(low_part, hadamard, preferred_element_type=jnp.float32)
    turned = turned * (1.0 / math.sqrt(BLOCK))
    return turned.reshape(row_count, -1)

def encode(values):
    row_count = values.shape[0]
    turned = rotate(values).reshape(row_count, -1, BLOCK)
    code_scales = (lax.optimization_barrier(jnp.mean(jnp.abs(turned), axis=-1)) + SCALE_EPS).astype(jnp.bfloat16)
    code_values = jnp.clip(turned / code_scales.astype(jnp.float32)[..., None], -CLIP_LEVEL, CLIP_LEVEL).astype(jnp.bfloat16)
    return (code_values.reshape(row_count, -1), code_scales)

def dequant(code_values, code_scales):
    reshaped = code_values.astype(jnp.float32).reshape(code_values.shape[:-1] + (code_scales.shape[-1], BLOCK))
    return reshaped * code_scales.astype(jnp.float32)[..., None]

def expand(code_values, code_scales):
    row_count = code_values.shape[0]
    hadamard = jnp.asarray(sylvester(BLOCK), jnp.bfloat16)
    mixed_rows = jnp.dot(code_values.reshape(-1, BLOCK), hadamard, preferred_element_type=jnp.float32)
    mixed_rows = mixed_rows.reshape(row_count, -1, BLOCK)
    factor = code_scales.astype(jnp.float32)[..., None] / math.sqrt(BLOCK)
    return (mixed_rows * factor).reshape(row_count, -1).astype(jnp.bfloat16)

def normalize(mid, ffn_gain):
    widened = mid.astype(jnp.float32)
    inverse = lax.rsqrt(lax.optimization_barrier(jnp.mean(widened * widened, axis=-1, keepdims=True)) + NORM_EPS)
    return widened * inverse * ffn_gain.astype(jnp.float32)

def hidden_units(rows_in, w_gate, w_up):
    gate_part = jnp.dot(rows_in, w_gate, preferred_element_type=jnp.float32)
    up_part = jnp.dot(rows_in, w_up, preferred_element_type=jnp.float32)
    return (jax.nn.silu(gate_part) * up_part).astype(jnp.bfloat16)

def reference(residual, context, w_out, ffn_gain, w_gate, w_up, w_down):
    model_width = residual.shape[1]
    head_inputs = context.reshape(ROWS, HEADS, HD).transpose(1, 0, 2)
    head_weights = w_out.reshape(HEADS, HD, model_width)

    def add_term(running_sum, operands):
        block_input, block_weight = operands
        partial_term = jnp.dot(block_input, block_weight, preferred_element_type=jnp.float32)
        code_values, code_scales = encode(partial_term)
        return (running_sum + dequant(code_values, code_scales), None)
    zero_sum = jnp.zeros((ROWS, model_width // BLOCK, BLOCK), jnp.float32)
    attn_sum, _ = lax.scan(add_term, zero_sum, (head_inputs, head_weights))
    mid = (residual.astype(jnp.float32) + rotate(attn_sum.reshape(ROWS, model_width))).astype(jnp.bfloat16)
    norm_values, norm_scales = encode(normalize(mid, ffn_gain))
    ffn_in = expand(norm_values, norm_scales)
    hidden = hidden_units(ffn_in, w_gate, w_up)
    block_inputs = hidden.reshape(ROWS, N_TENSOR, FF_DEV).transpose(1, 0, 2)
    block_weights = w_down.reshape(N_TENSOR, FF_DEV, model_width)
    ffn_sum, _ = lax.scan(add_term, zero_sum, (block_inputs, block_weights))
    layer_out = mid.astype(jnp.float32) + rotate(ffn_sum.reshape(ROWS, model_width))
    return layer_out.astype(jnp.bfloat16)
```

```python
import functools
import math

import jax
import jax.numpy as jnp
from jax import lax
from jax.experimental import pallas as pl
from jax.experimental.pallas import tpu as pltpu
from jax.sharding import PartitionSpec as P

BLOCK = 128
CLIP_LEVEL = 3.0
SCALE_EPS = 1e-06
NORM_EPS = 1e-05
CHUNKS = 4
PARTS = 2
MESH = pl.DeviceIdType.MESH
F32 = jnp.float32
BF16 = jnp.bfloat16
ROOT = 1.0 / math.sqrt(BLOCK)


def kernel(
    n, own, rows, blocks,
    res_ref, ctx_ref, wo_hbm, gain_ref, wg_hbm, wu_hbm, wd_hbm,
    out_ref,
    wo, wg, wu, wd, turn, s1, r1, s2, r2, s3, r3, resid, mid_ref, gath, lhs,
    wsem, s1s, s1r, s2s, s2r, s3s, s3r, gzs, gzr, gys, gyr, gcs, gcr,
):
    nh, nq = n // 2, n // 4
    bpc = blocks // CHUNKS
    cw = bpc * BLOCK
    per = own * bpc
    me = lax.axis_index("tensor")
    c = lax.rem(me, 2)
    y = lax.rem(me // 2, 2)
    q = me // 4
    core_dev = me + 1 - 2 * c
    y_dev = me + 2 - 4 * y

    def z_dev(k):
        return lax.rem(q + k, nq) * 4 + y * 2 + c

    def z_src(k):
        return lax.rem(q + nq - k, nq)

    wcopies = []
    for k in range(CHUNKS):
        cols = pl.ds(k * cw, cw)
        wcopies.append(pltpu.make_async_copy(wo_hbm.at[:, cols], wo.at[:, cols], wsem.at[k]))
    wcopies.append(pltpu.make_async_copy(wg_hbm, wg, wsem.at[CHUNKS]))
    wcopies.append(pltpu.make_async_copy(wu_hbm, wu, wsem.at[CHUNKS + 1]))
    wcopies.append(pltpu.make_async_copy(wd_hbm, wd, wsem.at[CHUNKS + 2]))
    for cp in wcopies:
        cp.start()

    barrier = pltpu.get_barrier_semaphore()
    for dev in [core_dev, y_dev] + [z_dev(k) for k in range(1, nq)]:
        pl.semaphore_signal(barrier, inc=1, device_id={"tensor": dev}, device_id_type=MESH)

    par = lax.broadcasted_iota(jnp.int32, (2 * BLOCK, BLOCK), 0) & lax.broadcasted_iota(
        jnp.int32, (2 * BLOCK, BLOCK), 1
    )
    par = par ^ (par >> 4)
    par = par ^ (par >> 2)
    par = par ^ (par >> 1)
    had2 = (1 - 2 * (par & 1)).astype(F32).astype(BF16)
    had = had2[:BLOCK]
    ones = jnp.ones((BLOCK, BLOCK), BF16)

    def rotate(v):
        high = v.astype(BF16)
        low = (v - high.astype(F32)).astype(BF16)
        return jnp.dot(jnp.concatenate([high, low], axis=1), had2, preferred_element_type=F32) * ROOT

    def coded(v):
        t = rotate(v)
        total = jnp.dot(jnp.abs(t).astype(BF16), ones, preferred_element_type=F32)
        scale = (total * (1.0 / BLOCK) + SCALE_EPS).astype(BF16).astype(F32)
        bound = scale * CLIP_LEVEL
        return jnp.clip(t, -bound, bound)

    sends = []

    def remote(src, dst, ssem, rsem, dev):
        cp = pltpu.make_async_remote_copy(
            src_ref=src, dst_ref=dst, send_sem=ssem, recv_sem=rsem,
            device_id={"tensor": dev}, device_id_type=MESH,
        )
        cp.start()
        sends.append(cp)
        return cp

    def term(p, k, left, w):
        x = jnp.dot(left, w[:, k * cw:(k + 1) * cw], preferred_element_type=F32)
        x = jnp.concatenate([x[:, b * BLOCK:(b + 1) * BLOCK] for b in range(bpc)], axis=0)
        v = coded(x)
        base = (k % 2) * rows * bpc
        for b in range(bpc):
            turn[pl.ds(base + b, rows, stride=bpc), :] = v[b * rows:(b + 1) * rows]
        for t in range(n):
            slot = (t % 2) * nh + (t // 2 % 2) * nq + t // 4
            s1[p, k, slot] = turn[base + t * per:base + (t + 1) * per, :].astype(BF16)

    def reduce_scatter(p, left, w, before):
        c1, c2, c3 = {}, {}, {}
        for step in range(CHUNKS + 2):
            k = step
            if k < CHUNKS:
                before(k)
                term(p, k, left, w)
                if p == 0 and k == 0:
                    pl.semaphore_wait(barrier, 1 + nq)
                c1[k] = remote(s1.at[p, k, pl.ds((1 - c) * nh, nh)], r1.at[p, k],
                               s1s.at[p, k], s1r.at[p, k], core_dev)
            k = step - 1
            if 0 <= k < CHUNKS:
                c1[k].wait_recv()
                s2[p, k] = (s1[p, k, pl.ds(c * nh, nh)].astype(F32) + r1[p, k].astype(F32)).astype(BF16)
                c2[k] = remote(s2.at[p, k, pl.ds((1 - y) * nq, nq)], r2.at[p, k],
                               s2s.at[p, k], s2r.at[p, k], y_dev)
            k = step - 2
            if 0 <= k < CHUNKS:
                c2[k].wait_recv()
                s3[p, k] = (s2[p, k, pl.ds(y * nq, nq)].astype(F32) + r2[p, k].astype(F32)).astype(BF16)
                for j in range(1, nq):
                    c3[k, j] = remote(s3.at[p, k, lax.rem(q + j, nq)], r3.at[p, k, j],
                                      s3s.at[p, k, j], s3r.at[p, k, j], z_dev(j))
        totals = []
        for k in range(CHUNKS):
            total = s3[p, k, q].astype(F32)
            for j in range(1, nq):
                c3[k, j].wait_recv()
                total = total + r3[p, k, j].astype(F32)
            totals.append(total)
        return jnp.concatenate(totals, axis=0)

    def before_out(k):
        wcopies[k].wait()

    res = res_ref[...].astype(F32)
    for b in range(blocks):
        resid[pl.ds((b // bpc) * per + b % bpc, own, stride=bpc), :] = res[:, b * BLOCK:(b + 1) * BLOCK]

    attn = reduce_scatter(0, ctx_ref[...], wo, before_out)
    mid = (resid[...] + rotate(attn)).astype(BF16).astype(F32)
    mid_ref[...] = mid
    mid4 = mid.reshape(CHUNKS, own, bpc, BLOCK)
    gain = gain_ref[...].astype(F32).reshape(CHUNKS, 1, bpc, BLOCK)
    squares = jnp.sum(jnp.sum(mid4 * mid4, axis=0), axis=(1, 2), keepdims=True)
    inverse = lax.rsqrt(squares * (1.0 / (blocks * BLOCK)) + NORM_EPS)
    normed = (mid4 * inverse[None] * gain).reshape(blocks * own, BLOCK)
    ffn_in = jnp.dot(coded(normed).astype(BF16), had, preferred_element_type=F32) * ROOT
    piece = own * blocks // PARTS
    cz, cy, cc = {}, {}, {}

    def share(a, slot, dev, ss, rs, i):
        return remote(gath.at[a, slot], gath.at[a, slot], ss.at[a, i], rs.at[a, i], dev)

    for a in range(PARTS):
        gath[a, me] = ffn_in[a * piece:(a + 1) * piece].astype(BF16)
        for k in range(1, nq):
            cz[a, k] = share(a, me, z_dev(k), gzs, gzr, k)
        cy[a, 0] = share(a, me, y_dev, gys, gyr, 0)
        cc[a, 0] = share(a, me, core_dev, gcs, gcr, 0)
    for a in range(PARTS):
        for k in range(1, nq):
            cz[a, k].wait_recv()
            slot = z_src(k) * 4 + y * 2 + c
            cy[a, k] = share(a, slot, y_dev, gys, gyr, k)
            cc[a, k] = share(a, slot, core_dev, gcs, gcr, k)
    for a in range(PARTS):
        for k in range(nq):
            cy[a, k].wait_recv()
            slot = z_src(k) * 4 + (1 - y) * 2 + c
            cc[a, nq + k] = share(a, slot, core_dev, gcs, gcr, nq + k)
    wcopies[CHUNKS].wait()
    wcopies[CHUNKS + 1].wait()
    gate = up = None
    group = CHUNKS // PARTS
    for a in range(PARTS):
        for k in range(nh):
            cc[a, k].wait_recv()
        for g in range(group):
            k = a * group + g
            base = k * rows * bpc
            for t in range(n):
                lhs[base + t * per:base + (t + 1) * per, :] = gath[a, t, g * per:(g + 1) * per, :].astype(F32)
            left = jnp.concatenate(
                [lhs[pl.ds(base + b, rows, stride=bpc), :].astype(BF16) for b in range(bpc)], axis=1
            )
            span = pl.ds(k * cw, cw)
            g_part = jnp.dot(left, wg[span, :], preferred_element_type=F32)
            u_part = jnp.dot(left, wu[span, :], preferred_element_type=F32)
            gate = g_part if gate is None else gate + g_part
            up = u_part if up is None else up + u_part
    hidden = (gate / (1.0 + jnp.exp(-gate)) * up).astype(BF16)

    def before_down(k):
        if k == 0:
            wcopies[CHUNKS + 2].wait()

    ffn = reduce_scatter(1, hidden, wd, before_down)
    resid[...] = mid_ref[...] + rotate(ffn)
    for b in range(blocks):
        row = resid[pl.ds((b // bpc) * per + b % bpc, own, stride=bpc), :]
        out_ref[:, b * BLOCK:(b + 1) * BLOCK] = row.astype(BF16)
    for cp in sends:
        cp.wait_send()


def local(residual, context, w_out, ffn_gain, w_gate, w_up, w_down):
    n = lax.axis_size("tensor")
    own, width = residual.shape
    rows = context.shape[0]
    blocks = width // BLOCK
    units = w_gate.shape[1]
    nh, nq = n // 2, n // 4
    per = own * blocks // CHUNKS
    piece = own * blocks // PARTS
    vmem = pl.BlockSpec(memory_space=pltpu.VMEM)
    hbm = pl.BlockSpec(memory_space=pl.ANY)
    dma = pltpu.SemaphoreType.DMA
    return pl.pallas_call(
        functools.partial(kernel, n, own, rows, blocks),
        out_shape=jax.ShapeDtypeStruct((own, width), BF16),
        in_specs=[vmem, vmem, hbm, vmem, hbm, hbm, hbm],
        out_specs=vmem,
        scratch_shapes=[
            pltpu.VMEM(w_out.shape, BF16),
            pltpu.VMEM((width, units), BF16),
            pltpu.VMEM((width, units), BF16),
            pltpu.VMEM(w_down.shape, BF16),
            pltpu.VMEM((2 * n * per, BLOCK), F32),
            pltpu.VMEM((2, CHUNKS, n, per, BLOCK), BF16),
            pltpu.VMEM((2, CHUNKS, nh, per, BLOCK), BF16),
            pltpu.VMEM((2, CHUNKS, nh, per, BLOCK), BF16),
            pltpu.VMEM((2, CHUNKS, nq, per, BLOCK), BF16),
            pltpu.VMEM((2, CHUNKS, nq, per, BLOCK), BF16),
            pltpu.VMEM((2, CHUNKS, nq, per, BLOCK), BF16),
            pltpu.VMEM((own * blocks, BLOCK), F32),
            pltpu.VMEM((own * blocks, BLOCK), F32),
            pltpu.VMEM((PARTS, n, piece, BLOCK), BF16),
            pltpu.VMEM((rows * blocks, BLOCK), F32),
            dma((CHUNKS + 3,)),
            dma((2, CHUNKS)), dma((2, CHUNKS)),
            dma((2, CHUNKS)), dma((2, CHUNKS)),
            dma((2, CHUNKS, nq)), dma((2, CHUNKS, nq)),
            dma((PARTS, nq)), dma((PARTS, nq)),
            dma((PARTS, nq)), dma((PARTS, nq)),
            dma((PARTS, nh)), dma((PARTS, nh)),
        ],
        compiler_params=pltpu.CompilerParams(
            collective_id=0, has_side_effects=True, vmem_limit_bytes=60 * 1024 * 1024
        ),
    )(residual, context, w_out, ffn_gain.reshape(blocks, BLOCK), w_gate, w_up, w_down)


def solution(mesh):
    return jax.shard_map(
        local,
        mesh=mesh,
        in_specs=(
            P(("groups", "tensor"), None),
            P("groups", "tensor"),
            P("tensor", None),
            P(),
            P(None, "tensor"),
            P(None, "tensor"),
            P("tensor", None),
        ),
        out_specs=P(("groups", "tensor"), None),
        check_vma=False,
    )
```

```python
import functools
import math

import jax
import jax.numpy as jnp
from jax import lax
from jax.experimental import pallas as pl
from jax.experimental.pallas import tpu as pltpu
from jax.sharding import PartitionSpec as P

BLOCK = 128
CLIP_LEVEL = 3.0
SCALE_EPS = 1e-06
NORM_EPS = 1e-05
CHUNKS = 4
PARTS = 2
MESH = pl.DeviceIdType.MESH
F32 = jnp.float32
BF16 = jnp.bfloat16
NT = (((1,), (1,)), ((), ()))
ROOT = 1.0 / math.sqrt(BLOCK)


def kernel(
    n, own, rows, blocks,
    res_ref, ctx_ref, wo_hbm, gain_ref, wg_hbm, wu_hbm, wd_hbm,
    out_ref,
    wo, wg, wu, wd, turn, s1, r1, s2, r2, s3, r3, resid, mid_ref, gath, lhs,
    wsem, s1s, s1r, s2s, s2r, s3s, s3r, gzs, gzr, gys, gyr, gcs, gcr,
):
    nh, nq = n // 2, n // 4
    bpc = blocks // CHUNKS
    cw = bpc * BLOCK
    per = own * bpc
    me = lax.axis_index("tensor")
    c = lax.rem(me, 2)
    y = lax.rem(me // 2, 2)
    q = me // 4
    core_dev = me + 1 - 2 * c
    y_dev = me + 2 - 4 * y

    def z_dev(k):
        return lax.rem(q + k, nq) * 4 + y * 2 + c

    def z_src(k):
        return lax.rem(q + nq - k, nq)

    wcopies = []
    for k in range(CHUNKS):
        cols = pl.ds(k * cw, cw)
        wcopies.append(pltpu.make_async_copy(wo_hbm.at[:, cols], wo.at[:, cols], wsem.at[k]))
    wcopies.append(pltpu.make_async_copy(wg_hbm, wg, wsem.at[CHUNKS]))
    wcopies.append(pltpu.make_async_copy(wu_hbm, wu, wsem.at[CHUNKS + 1]))
    wcopies.append(pltpu.make_async_copy(wd_hbm, wd, wsem.at[CHUNKS + 2]))
    for cp in wcopies:
        cp.start()

    barrier = pltpu.get_barrier_semaphore()
    for dev in [core_dev, y_dev] + [z_dev(k) for k in range(1, nq)]:
        pl.semaphore_signal(barrier, inc=1, device_id={"tensor": dev}, device_id_type=MESH)

    par = lax.broadcasted_iota(jnp.int32, (2 * BLOCK, BLOCK), 0) & lax.broadcasted_iota(
        jnp.int32, (2 * BLOCK, BLOCK), 1
    )
    par = par ^ (par >> 4)
    par = par ^ (par >> 2)
    par = par ^ (par >> 1)
    had2 = (1 - 2 * (par & 1)).astype(F32).astype(BF16)
    had = had2[:BLOCK]
    ones = jnp.ones((BLOCK, BLOCK), BF16)

    def rotate(v):
        high = v.astype(BF16)
        low = (v - high.astype(F32)).astype(BF16)
        return jnp.dot(jnp.concatenate([high, low], axis=1), had2, preferred_element_type=F32) * ROOT

    def coded(v):
        t = rotate(v)
        total = jnp.dot(jnp.abs(t).astype(BF16), ones, preferred_element_type=F32)
        scale = (total * (1.0 / BLOCK) + SCALE_EPS).astype(BF16).astype(F32)
        bound = scale * CLIP_LEVEL
        return jnp.clip(t, -bound, bound)

    sends = []

    def remote(src, dst, ssem, rsem, dev):
        cp = pltpu.make_async_remote_copy(
            src_ref=src, dst_ref=dst, send_sem=ssem, recv_sem=rsem,
            device_id={"tensor": dev}, device_id_type=MESH,
        )
        cp.start()
        sends.append(cp)
        return cp

    def term(p, k, left, w):
        x = jnp.dot(left, w[:, k * cw:(k + 1) * cw], preferred_element_type=F32)
        x = jnp.concatenate([x[:, b * BLOCK:(b + 1) * BLOCK] for b in range(bpc)], axis=0)
        v = coded(x)
        base = (k % 2) * rows * bpc
        for b in range(bpc):
            turn[pl.ds(base + b, rows, stride=bpc), :] = v[b * rows:(b + 1) * rows]
        for t in range(n):
            slot = (t % 2) * nh + (t // 2 % 2) * nq + t // 4
            s1[p, k, slot] = turn[base + t * per:base + (t + 1) * per, :].astype(BF16)

    def reduce_scatter(p, left, w, before):
        c1, c2, c3 = {}, {}, {}
        for step in range(CHUNKS + 2):
            k = step
            if k < CHUNKS:
                before(k)
                term(p, k, left, w)
                if p == 0 and k == 0:
                    pl.semaphore_wait(barrier, 1 + nq)
                c1[k] = remote(s1.at[p, k, pl.ds((1 - c) * nh, nh)], r1.at[p, k],
                               s1s.at[p, k], s1r.at[p, k], core_dev)
            k = step - 1
            if 0 <= k < CHUNKS:
                c1[k].wait_recv()
                s2[p, k] = (s1[p, k, pl.ds(c * nh, nh)].astype(F32) + r1[p, k].astype(F32)).astype(BF16)
                c2[k] = remote(s2.at[p, k, pl.ds((1 - y) * nq, nq)], r2.at[p, k],
                               s2s.at[p, k], s2r.at[p, k], y_dev)
            k = step - 2
            if 0 <= k < CHUNKS:
                c2[k].wait_recv()
                s3[p, k] = (s2[p, k, pl.ds(y * nq, nq)].astype(F32) + r2[p, k].astype(F32)).astype(BF16)
                for j in range(1, nq):
                    c3[k, j] = remote(s3.at[p, k, lax.rem(q + j, nq)], r3.at[p, k, j],
                                      s3s.at[p, k, j], s3r.at[p, k, j], z_dev(j))
        totals = []
        for k in range(CHUNKS):
            total = s3[p, k, q].astype(F32)
            for j in range(1, nq):
                c3[k, j].wait_recv()
                total = total + r3[p, k, j].astype(F32)
            totals.append(total)
        return jnp.concatenate(totals, axis=0)

    def before_out(k):
        wcopies[k].wait()

    res = res_ref[...].astype(F32)
    for b in range(blocks):
        resid[pl.ds((b // bpc) * per + b % bpc, own, stride=bpc), :] = res[:, b * BLOCK:(b + 1) * BLOCK]

    attn = reduce_scatter(0, ctx_ref[...], wo, before_out)
    mid = (resid[...] + rotate(attn)).astype(BF16).astype(F32)
    mid_ref[...] = mid
    mid4 = mid.reshape(CHUNKS, own, bpc, BLOCK)
    gain = gain_ref[...].astype(F32).reshape(CHUNKS, 1, bpc, BLOCK)
    squares = jnp.sum(jnp.sum(mid4 * mid4, axis=0), axis=(1, 2), keepdims=True)
    inverse = lax.rsqrt(squares * (1.0 / (blocks * BLOCK)) + NORM_EPS)
    normed = (mid4 * inverse[None] * gain).reshape(blocks * own, BLOCK)
    ffn_in = jnp.dot(coded(normed).astype(BF16), had, preferred_element_type=F32) * ROOT
    piece = own * blocks // PARTS
    cz, cy, cc = {}, {}, {}

    def share(a, slot, dev, ss, rs, i):
        return remote(gath.at[a, slot], gath.at[a, slot], ss.at[a, i], rs.at[a, i], dev)

    for a in range(PARTS):
        gath[a, me] = ffn_in[a * piece:(a + 1) * piece].astype(BF16)
        for k in range(1, nq):
            cz[a, k] = share(a, me, z_dev(k), gzs, gzr, k)
        cy[a, 0] = share(a, me, y_dev, gys, gyr, 0)
        cc[a, 0] = share(a, me, core_dev, gcs, gcr, 0)
    for a in range(PARTS):
        for k in range(1, nq):
            cz[a, k].wait_recv()
            slot = z_src(k) * 4 + y * 2 + c
            cy[a, k] = share(a, slot, y_dev, gys, gyr, k)
            cc[a, k] = share(a, slot, core_dev, gcs, gcr, k)
    for a in range(PARTS):
        for k in range(nq):
            cy[a, k].wait_recv()
            slot = z_src(k) * 4 + (1 - y) * 2 + c
            cc[a, nq + k] = share(a, slot, core_dev, gcs, gcr, nq + k)
    wcopies[CHUNKS].wait()
    wcopies[CHUNKS + 1].wait()
    gate = up = None
    group = CHUNKS // PARTS
    for a in range(PARTS):
        for k in range(nh):
            cc[a, k].wait_recv()
        for g in range(group):
            k = a * group + g
            base = k * rows * bpc
            for t in range(n):
                lhs[base + t * per:base + (t + 1) * per, :] = gath[a, t, g * per:(g + 1) * per, :].astype(F32)
            left = jnp.concatenate(
                [lhs[pl.ds(base + b, rows, stride=bpc), :].astype(BF16) for b in range(bpc)], axis=1
            )
            span = pl.ds(k * cw, cw)
            g_part = lax.dot_general(left, wg[:, span], NT, preferred_element_type=F32)
            u_part = lax.dot_general(left, wu[:, span], NT, preferred_element_type=F32)
            gate = g_part if gate is None else gate + g_part
            up = u_part if up is None else up + u_part
    hidden = (gate / (1.0 + jnp.exp(-gate)) * up).astype(BF16)

    def before_down(k):
        if k == 0:
            wcopies[CHUNKS + 2].wait()

    ffn = reduce_scatter(1, hidden, wd, before_down)
    resid[...] = mid_ref[...] + rotate(ffn)
    for b in range(blocks):
        row = resid[pl.ds((b // bpc) * per + b % bpc, own, stride=bpc), :]
        out_ref[:, b * BLOCK:(b + 1) * BLOCK] = row.astype(BF16)
    for cp in sends:
        cp.wait_send()


def local(residual, context, w_out, ffn_gain, w_gate, w_up, w_down):
    n = lax.axis_size("tensor")
    own, width = residual.shape
    rows = context.shape[0]
    blocks = width // BLOCK
    units = w_gate.shape[1]
    nh, nq = n // 2, n // 4
    per = own * blocks // CHUNKS
    piece = own * blocks // PARTS
    vmem = pl.BlockSpec(memory_space=pltpu.VMEM)
    hbm = pl.BlockSpec(memory_space=pl.ANY)
    dma = pltpu.SemaphoreType.DMA
    return pl.pallas_call(
        functools.partial(kernel, n, own, rows, blocks),
        out_shape=jax.ShapeDtypeStruct((own, width), BF16),
        in_specs=[vmem, vmem, hbm, vmem, hbm, hbm, hbm],
        out_specs=vmem,
        scratch_shapes=[
            pltpu.VMEM(w_out.shape, BF16),
            pltpu.VMEM((units, width), BF16),
            pltpu.VMEM((units, width), BF16),
            pltpu.VMEM(w_down.shape, BF16),
            pltpu.VMEM((2 * n * per, BLOCK), F32),
            pltpu.VMEM((2, CHUNKS, n, per, BLOCK), BF16),
            pltpu.VMEM((2, CHUNKS, nh, per, BLOCK), BF16),
            pltpu.VMEM((2, CHUNKS, nh, per, BLOCK), BF16),
            pltpu.VMEM((2, CHUNKS, nq, per, BLOCK), BF16),
            pltpu.VMEM((2, CHUNKS, nq, per, BLOCK), BF16),
            pltpu.VMEM((2, CHUNKS, nq, per, BLOCK), BF16),
            pltpu.VMEM((own * blocks, BLOCK), F32),
            pltpu.VMEM((own * blocks, BLOCK), F32),
            pltpu.VMEM((PARTS, n, piece, BLOCK), BF16),
            pltpu.VMEM((rows * blocks, BLOCK), F32),
            dma((CHUNKS + 3,)),
            dma((2, CHUNKS)), dma((2, CHUNKS)),
            dma((2, CHUNKS)), dma((2, CHUNKS)),
            dma((2, CHUNKS, nq)), dma((2, CHUNKS, nq)),
            dma((PARTS, nq)), dma((PARTS, nq)),
            dma((PARTS, nq)), dma((PARTS, nq)),
            dma((PARTS, nh)), dma((PARTS, nh)),
        ],
        compiler_params=pltpu.CompilerParams(
            collective_id=0, has_side_effects=True, vmem_limit_bytes=60 * 1024 * 1024
        ),
    )(residual, context, w_out, ffn_gain.reshape(blocks, BLOCK), w_gate.T, w_up.T, w_down)


def solution(mesh):
    return jax.shard_map(
        local,
        mesh=mesh,
        in_specs=(
            P(("groups", "tensor"), None),
            P("groups", "tensor"),
            P("tensor", None),
            P(),
            P(None, "tensor"),
            P(None, "tensor"),
            P("tensor", None),
        ),
        out_specs=P(("groups", "tensor"), None),
        check_vma=False,
    )
```

```python
import functools
import math

import jax
import jax.numpy as jnp
from jax import lax
from jax.experimental import pallas as pl
from jax.experimental.pallas import tpu as pltpu
from jax.sharding import PartitionSpec as P

BLOCK = 128
CLIP_LEVEL = 3.0
SCALE_EPS = 1e-06
NORM_EPS = 1e-05
CHUNKS = 4
PARTS = 2
MESH = pl.DeviceIdType.MESH
F32 = jnp.float32
BF16 = jnp.bfloat16
NT = (((1,), (1,)), ((), ()))
ROOT = 1.0 / math.sqrt(BLOCK)


def kernel(
    n, own, rows, blocks,
    res_ref, ctx_ref, wo_hbm, gain_ref, wg_hbm, wu_hbm, wd_hbm,
    out_ref,
    wo, wg, wu, wd, turn, s1, r1, s2, r2, resid, mid_ref, gath, lhs,
    wsem, s1s, s1r, s2s, s2r, gds, gdr, gcs, gcr,
):
    nh = n // 2
    bpc = blocks // CHUNKS
    cw = bpc * BLOCK
    per = own * bpc
    me = lax.axis_index("tensor")
    c = lax.rem(me, 2)
    chip = me // 2
    core_dev = me + 1 - 2 * c

    def far(k):
        return lax.rem(chip + k, nh) * 2 + c

    def source(k):
        return lax.rem(chip + nh - k, nh) * 2 + c

    wcopies = []
    for k in range(CHUNKS):
        cols = pl.ds(k * cw, cw)
        wcopies.append(pltpu.make_async_copy(wo_hbm.at[:, cols], wo.at[:, cols], wsem.at[k]))
    wcopies.append(pltpu.make_async_copy(wg_hbm, wg, wsem.at[CHUNKS]))
    wcopies.append(pltpu.make_async_copy(wu_hbm, wu, wsem.at[CHUNKS + 1]))
    wcopies.append(pltpu.make_async_copy(wd_hbm, wd, wsem.at[CHUNKS + 2]))
    for cp in wcopies:
        cp.start()

    barrier = pltpu.get_barrier_semaphore()
    for dev in [core_dev] + [far(k) for k in range(1, nh)]:
        pl.semaphore_signal(barrier, inc=1, device_id={"tensor": dev}, device_id_type=MESH)

    par = lax.broadcasted_iota(jnp.int32, (2 * BLOCK, BLOCK), 0) & lax.broadcasted_iota(
        jnp.int32, (2 * BLOCK, BLOCK), 1
    )
    par = par ^ (par >> 4)
    par = par ^ (par >> 2)
    par = par ^ (par >> 1)
    had2 = (1 - 2 * (par & 1)).astype(F32).astype(BF16)
    had = had2[:BLOCK]
    ones = jnp.ones((BLOCK, BLOCK), BF16)

    def rotate(v):
        high = v.astype(BF16)
        low = (v - high.astype(F32)).astype(BF16)
        return jnp.dot(jnp.concatenate([high, low], axis=1), had2, preferred_element_type=F32) * ROOT

    def coded(v):
        t = rotate(v)
        total = jnp.dot(jnp.abs(t).astype(BF16), ones, preferred_element_type=F32)
        scale = (total * (1.0 / BLOCK) + SCALE_EPS).astype(BF16).astype(F32)
        bound = scale * CLIP_LEVEL
        return jnp.clip(t, -bound, bound)

    sends = []

    def remote(src, dst, ssem, rsem, dev):
        cp = pltpu.make_async_remote_copy(
            src_ref=src, dst_ref=dst, send_sem=ssem, recv_sem=rsem,
            device_id={"tensor": dev}, device_id_type=MESH,
        )
        cp.start()
        sends.append(cp)
        return cp

    def term(p, k, left, w):
        x = jnp.dot(left, w[:, k * cw:(k + 1) * cw], preferred_element_type=F32)
        x = jnp.concatenate([x[:, b * BLOCK:(b + 1) * BLOCK] for b in range(bpc)], axis=0)
        v = coded(x)
        base = (k % 2) * rows * bpc
        for b in range(bpc):
            turn[pl.ds(base + b, rows, stride=bpc), :] = v[b * rows:(b + 1) * rows]
        for t in range(n):
            slot = (t % 2) * nh + t // 2
            s1[p, k, slot] = turn[base + t * per:base + (t + 1) * per, :].astype(BF16)

    def reduce_scatter(p, left, w, before):
        c1, c2 = {}, {}
        for step in range(CHUNKS + 1):
            k = step
            if k < CHUNKS:
                before(k)
                term(p, k, left, w)
                if p == 0 and k == 0:
                    pl.semaphore_wait(barrier, nh)
                c1[k] = remote(s1.at[p, k, pl.ds((1 - c) * nh, nh)], r1.at[p, k],
                               s1s.at[p, k], s1r.at[p, k], core_dev)
            k = step - 1
            if k >= 0:
                c1[k].wait_recv()
                s2[p, k] = (s1[p, k, pl.ds(c * nh, nh)].astype(F32) + r1[p, k].astype(F32)).astype(BF16)
                for j in range(1, nh):
                    c2[k, j] = remote(s2.at[p, k, lax.rem(chip + j, nh)], r2.at[p, k, j],
                                      s2s.at[p, k, j], s2r.at[p, k, j], far(j))
        totals = []
        for k in range(CHUNKS):
            total = s2[p, k, chip].astype(F32)
            for j in range(1, nh):
                c2[k, j].wait_recv()
                total = total + r2[p, k, j].astype(F32)
            totals.append(total)
        return jnp.concatenate(totals, axis=0)

    def before_out(k):
        wcopies[k].wait()

    res = res_ref[...].astype(F32)
    for b in range(blocks):
        resid[pl.ds((b // bpc) * per + b % bpc, own, stride=bpc), :] = res[:, b * BLOCK:(b + 1) * BLOCK]

    attn = reduce_scatter(0, ctx_ref[...], wo, before_out)
    mid = (resid[...] + rotate(attn)).astype(BF16).astype(F32)
    mid_ref[...] = mid
    mid4 = mid.reshape(CHUNKS, own, bpc, BLOCK)
    gain = gain_ref[...].astype(F32).reshape(CHUNKS, 1, bpc, BLOCK)
    squares = jnp.sum(jnp.sum(mid4 * mid4, axis=0), axis=(1, 2), keepdims=True)
    inverse = lax.rsqrt(squares * (1.0 / (blocks * BLOCK)) + NORM_EPS)
    normed = (mid4 * inverse[None] * gain).reshape(blocks * own, BLOCK)
    ffn_in = jnp.dot(coded(normed).astype(BF16), had, preferred_element_type=F32) * ROOT
    piece = own * blocks // PARTS
    cd, cc = {}, {}
    group = CHUNKS // PARTS

    def share(a, slot, dev, ss, rs, i):
        return remote(gath.at[a, slot], gath.at[a, slot], ss.at[a, i], rs.at[a, i], dev)

    def place(a, slot):
        for g in range(group):
            start = pl.multiple_of((a * group + g) * rows * bpc + slot * per, per)
            lhs[pl.ds(start, per), :] = gath[a, slot, g * per:(g + 1) * per, :].astype(F32)

    for a in range(PARTS):
        gath[a, me] = ffn_in[a * piece:(a + 1) * piece].astype(BF16)
        for k in range(1, nh):
            cd[a, k] = share(a, me, far(k), gds, gdr, k)
        cc[a, 0] = share(a, me, core_dev, gcs, gcr, 0)
    for a in range(PARTS):
        place(a, me)
        for k in range(1, nh):
            cd[a, k].wait_recv()
            cc[a, k] = share(a, source(k), core_dev, gcs, gcr, k)
            place(a, source(k))
    wcopies[CHUNKS].wait()
    wcopies[CHUNKS + 1].wait()
    gate = up = None
    for a in range(PARTS):
        for k in range(nh):
            cc[a, k].wait_recv()
            place(a, source(k) + 1 - 2 * c)
        for g in range(group):
            k = a * group + g
            base = k * rows * bpc
            left = jnp.concatenate(
                [lhs[pl.ds(base + b, rows, stride=bpc), :].astype(BF16) for b in range(bpc)], axis=1
            )
            span = pl.ds(k * cw, cw)
            g_part = lax.dot_general(left, wg[:, span], NT, preferred_element_type=F32)
            u_part = lax.dot_general(left, wu[:, span], NT, preferred_element_type=F32)
            gate = g_part if gate is None else gate + g_part
            up = u_part if up is None else up + u_part
    hidden = (gate / (1.0 + jnp.exp(-gate)) * up).astype(BF16)

    def before_down(k):
        if k == 0:
            wcopies[CHUNKS + 2].wait()

    ffn = reduce_scatter(1, hidden, wd, before_down)
    resid[...] = mid_ref[...] + rotate(ffn)
    for b in range(blocks):
        row = resid[pl.ds((b // bpc) * per + b % bpc, own, stride=bpc), :]
        out_ref[:, b * BLOCK:(b + 1) * BLOCK] = row.astype(BF16)
    for cp in sends:
        cp.wait_send()


def local(residual, context, w_out, ffn_gain, w_gate, w_up, w_down):
    n = lax.axis_size("tensor")
    own, width = residual.shape
    rows = context.shape[0]
    blocks = width // BLOCK
    units = w_gate.shape[1]
    nh = n // 2
    per = own * blocks // CHUNKS
    piece = own * blocks // PARTS
    vmem = pl.BlockSpec(memory_space=pltpu.VMEM)
    hbm = pl.BlockSpec(memory_space=pl.ANY)
    dma = pltpu.SemaphoreType.DMA
    return pl.pallas_call(
        functools.partial(kernel, n, own, rows, blocks),
        out_shape=jax.ShapeDtypeStruct((own, width), BF16),
        in_specs=[vmem, vmem, hbm, vmem, hbm, hbm, hbm],
        out_specs=vmem,
        scratch_shapes=[
            pltpu.VMEM(w_out.shape, BF16),
            pltpu.VMEM((units, width), BF16),
            pltpu.VMEM((units, width), BF16),
            pltpu.VMEM(w_down.shape, BF16),
            pltpu.VMEM((2 * n * per, BLOCK), F32),
            pltpu.VMEM((2, CHUNKS, n, per, BLOCK), BF16),
            pltpu.VMEM((2, CHUNKS, nh, per, BLOCK), BF16),
            pltpu.VMEM((2, CHUNKS, nh, per, BLOCK), BF16),
            pltpu.VMEM((2, CHUNKS, nh, per, BLOCK), BF16),
            pltpu.VMEM((own * blocks, BLOCK), F32),
            pltpu.VMEM((own * blocks, BLOCK), F32),
            pltpu.VMEM((PARTS, n, piece, BLOCK), BF16),
            pltpu.VMEM((rows * blocks, BLOCK), F32),
            dma((CHUNKS + 3,)),
            dma((2, CHUNKS)), dma((2, CHUNKS)),
            dma((2, CHUNKS, nh)), dma((2, CHUNKS, nh)),
            dma((PARTS, nh)), dma((PARTS, nh)),
            dma((PARTS, nh)), dma((PARTS, nh)),
        ],
        compiler_params=pltpu.CompilerParams(
            collective_id=0, has_side_effects=True, vmem_limit_bytes=60 * 1024 * 1024
        ),
    )(residual, context, w_out, ffn_gain.reshape(blocks, BLOCK), w_gate.T, w_up.T, w_down)


def solution(mesh):
    return jax.shard_map(
        local,
        mesh=mesh,
        in_specs=(
            P(("groups", "tensor"), None),
            P("groups", "tensor"),
            P("tensor", None),
            P(),
            P(None, "tensor"),
            P(None, "tensor"),
            P("tensor", None),
        ),
        out_specs=P(("groups", "tensor"), None),
        check_vma=False,
    )
```

```python
import functools
import math

import jax
import jax.numpy as jnp
from jax import lax
from jax.experimental import pallas as pl
from jax.experimental.pallas import tpu as pltpu
from jax.sharding import PartitionSpec as P

BLOCK = 128
CLIP_LEVEL = 3.0
SCALE_EPS = 1e-06
NORM_EPS = 1e-05
CHUNKS = 4
PARTS = 2
MESH = pl.DeviceIdType.MESH
F32 = jnp.float32
BF16 = jnp.bfloat16
NT = (((1,), (1,)), ((), ()))


def partner_order(count):
    return range(count - 1, 0, -1)


ROOT = 1.0 / math.sqrt(BLOCK)


def kernel(
    n, own, rows, blocks,
    res_hbm, ctx_hbm, wo_hbm, gain_hbm, wg_hbm, wu_hbm, wd_hbm,
    out_ref,
    res_ref, ctx_ref, gain_ref, wo, wg, wu, wd, turn, s1, r1, s2, r2, resid, mid_ref, gath, lhs,
    wsem, s1s, s1r, s2s, s2r, gds, gdr, gcs, gcr,
):
    nh = n // 2
    bpc = blocks // CHUNKS
    cw = bpc * BLOCK
    per = own * bpc
    me = lax.axis_index("tensor")
    c = lax.rem(me, 2)
    chip = me // 2
    core_dev = me + 1 - 2 * c

    def flip(k):
        other, bit = chip, 1
        while bit < nh:
            if k & bit:
                other = other + bit * (1 - 2 * lax.rem(chip // bit, 2))
            bit *= 2
        return other

    def far(k):
        return flip(k) * 2 + c

    source = far

    barrier = pltpu.get_barrier_semaphore()
    for dev in [core_dev] + [far(k) for k in partner_order(nh)]:
        pl.semaphore_signal(barrier, inc=1, device_id={"tensor": dev}, device_id_type=MESH)

    small = []
    for i, (src, dst) in enumerate(((ctx_hbm, ctx_ref), (res_hbm, res_ref), (gain_hbm, gain_ref))):
        small.append(pltpu.make_async_copy(src, dst, wsem.at[CHUNKS + 3 + i]))
    small[0].start()
    wcopies = []
    for k in range(CHUNKS):
        cols = pl.ds(k * cw, cw)
        wcopies.append(pltpu.make_async_copy(wo_hbm.at[:, cols], wo.at[:, cols], wsem.at[k]))
    wcopies.append(pltpu.make_async_copy(wg_hbm, wg, wsem.at[CHUNKS]))
    wcopies.append(pltpu.make_async_copy(wu_hbm, wu, wsem.at[CHUNKS + 1]))
    wcopies.append(pltpu.make_async_copy(wd_hbm, wd, wsem.at[CHUNKS + 2]))
    for cp in wcopies[:CHUNKS] + small[1:]:
        cp.start()

    par = lax.broadcasted_iota(jnp.int32, (2 * BLOCK, BLOCK), 0) & lax.broadcasted_iota(
        jnp.int32, (2 * BLOCK, BLOCK), 1
    )
    par = par ^ (par >> 4)
    par = par ^ (par >> 2)
    par = par ^ (par >> 1)
    had2 = (1 - 2 * (par & 1)).astype(F32).astype(BF16)
    had = had2[:BLOCK]
    ones = jnp.ones((BLOCK, BLOCK), BF16)

    def rotate(v):
        high = v.astype(BF16)
        low = (v - high.astype(F32)).astype(BF16)
        return jnp.dot(jnp.concatenate([high, low], axis=1), had2, preferred_element_type=F32) * ROOT

    def coded(v):
        t = rotate(v)
        total = jnp.dot(jnp.abs(t).astype(BF16), ones, preferred_element_type=F32)
        scale = (total * (1.0 / BLOCK) + SCALE_EPS).astype(BF16).astype(F32)
        bound = scale * CLIP_LEVEL
        return jnp.clip(t, -bound, bound)

    sends = []

    def remote(src, dst, ssem, rsem, dev):
        cp = pltpu.make_async_remote_copy(
            src_ref=src, dst_ref=dst, send_sem=ssem, recv_sem=rsem,
            device_id={"tensor": dev}, device_id_type=MESH,
        )
        cp.start()
        sends.append(cp)
        return cp

    def term(p, k, left, w):
        x = jnp.dot(left, w[:, k * cw:(k + 1) * cw], preferred_element_type=F32)
        x = jnp.concatenate([x[:, b * BLOCK:(b + 1) * BLOCK] for b in range(bpc)], axis=0)
        v = coded(x)
        base = (k % 2) * rows * bpc
        for b in range(bpc):
            turn[pl.ds(base + b, rows, stride=bpc), :] = v[b * rows:(b + 1) * rows]
        for t in range(n):
            slot = (t % 2) * nh + t // 2
            s1[p, k, slot] = turn[base + t * per:base + (t + 1) * per, :].astype(BF16)

    def reduce_scatter(p, left, w, before, between):
        c1, c2 = {}, {}
        for step in range(CHUNKS + 1):
            k = step
            if k < CHUNKS:
                before(k)
                term(p, k, left, w)
                if p == 0 and k == 0:
                    pl.semaphore_wait(barrier, nh)
                c1[k] = remote(s1.at[p, k, pl.ds((1 - c) * nh, nh)], r1.at[p, k],
                               s1s.at[p, k], s1r.at[p, k], core_dev)
            k = step - 1
            if k >= 0:
                c1[k].wait_recv()
                s2[p, k] = (s1[p, k, pl.ds(c * nh, nh)].astype(F32) + r1[p, k].astype(F32)).astype(BF16)
                for j in partner_order(nh):
                    c2[k, j] = remote(s2.at[p, k, flip(j)], r2.at[p, k, j],
                                      s2s.at[p, k, j], s2r.at[p, k, j], far(j))
        between()
        totals = []
        for k in range(CHUNKS):
            total = s2[p, k, chip].astype(F32)
            for j in range(1, nh):
                c2[k, j].wait_recv()
                total = total + r2[p, k, j].astype(F32)
            totals.append(total)
        return jnp.concatenate(totals, axis=0)

    def before_out(k):
        wcopies[k].wait()
        if k == CHUNKS - 1:
            for cp in wcopies[CHUNKS:]:
                cp.start()

    def spread_residual():
        small[1].wait()
        small[2].wait()
        res = res_ref[...].astype(F32)
        for b in range(blocks):
            resid[pl.ds((b // bpc) * per + b % bpc, own, stride=bpc), :] = res[:, b * BLOCK:(b + 1) * BLOCK]

    small[0].wait()
    attn = reduce_scatter(0, ctx_ref[...], wo, before_out, spread_residual)
    mid = (resid[...] + rotate(attn)).astype(BF16).astype(F32)
    mid_ref[...] = mid
    mid4 = mid.reshape(CHUNKS, own, bpc, BLOCK)
    gain = gain_ref[...].astype(F32).reshape(CHUNKS, 1, bpc, BLOCK)
    squares = jnp.sum(jnp.sum(mid4 * mid4, axis=0), axis=(1, 2), keepdims=True)
    inverse = lax.rsqrt(squares * (1.0 / (blocks * BLOCK)) + NORM_EPS)
    normed = (mid4 * inverse[None] * gain).reshape(blocks * own, BLOCK)
    ffn_in = jnp.dot(coded(normed).astype(BF16), had, preferred_element_type=F32) * ROOT
    piece = own * blocks // PARTS
    cd, cc = {}, {}
    group = CHUNKS // PARTS

    def share(a, slot, dev, ss, rs, i):
        return remote(gath.at[a, slot], gath.at[a, slot], ss.at[a, i], rs.at[a, i], dev)

    def place(a, slot):
        for g in range(group):
            start = pl.multiple_of((a * group + g) * rows * bpc + slot * per, per)
            lhs[pl.ds(start, per), :] = gath[a, slot, g * per:(g + 1) * per, :].astype(F32)

    for a in range(PARTS):
        gath[a, me] = ffn_in[a * piece:(a + 1) * piece].astype(BF16)
        for k in partner_order(nh):
            cd[a, k] = share(a, me, far(k), gds, gdr, k)
        cc[a, 0] = share(a, me, core_dev, gcs, gcr, 0)
    for a in range(PARTS):
        place(a, me)
        for k in range(1, nh):
            cd[a, k].wait_recv()
            cc[a, k] = share(a, source(k), core_dev, gcs, gcr, k)
            place(a, source(k))
    wcopies[CHUNKS].wait()
    wcopies[CHUNKS + 1].wait()
    gate = up = None
    for a in range(PARTS):
        for k in range(nh):
            cc[a, k].wait_recv()
            place(a, source(k) + 1 - 2 * c)
        for g in range(group):
            k = a * group + g
            base = k * rows * bpc
            left = jnp.concatenate(
                [lhs[pl.ds(base + b, rows, stride=bpc), :].astype(BF16) for b in range(bpc)], axis=1
            )
            span = pl.ds(k * cw, cw)
            g_part = lax.dot_general(left, wg[:, span], NT, preferred_element_type=F32)
            u_part = lax.dot_general(left, wu[:, span], NT, preferred_element_type=F32)
            gate = g_part if gate is None else gate + g_part
            up = u_part if up is None else up + u_part
    hidden = (gate / (1.0 + jnp.exp(-gate)) * up).astype(BF16)

    def before_down(k):
        if k == 0:
            wcopies[CHUNKS + 2].wait()

    ffn = reduce_scatter(1, hidden, wd, before_down, lambda: None)
    resid[...] = mid_ref[...] + rotate(ffn)
    for b in range(blocks):
        row = resid[pl.ds((b // bpc) * per + b % bpc, own, stride=bpc), :]
        out_ref[:, b * BLOCK:(b + 1) * BLOCK] = row.astype(BF16)
    for cp in sends:
        cp.wait_send()


def local(residual, context, w_out, ffn_gain, w_gate, w_up, w_down):
    n = lax.axis_size("tensor")
    own, width = residual.shape
    rows = context.shape[0]
    blocks = width // BLOCK
    units = w_gate.shape[1]
    nh = n // 2
    per = own * blocks // CHUNKS
    piece = own * blocks // PARTS
    vmem = pl.BlockSpec(memory_space=pltpu.VMEM)
    hbm = pl.BlockSpec(memory_space=pl.ANY)
    dma = pltpu.SemaphoreType.DMA
    return pl.pallas_call(
        functools.partial(kernel, n, own, rows, blocks),
        out_shape=jax.ShapeDtypeStruct((own, width), BF16),
        in_specs=[hbm] * 7,
        out_specs=vmem,
        scratch_shapes=[
            pltpu.VMEM(residual.shape, BF16),
            pltpu.VMEM(context.shape, BF16),
            pltpu.VMEM((blocks, BLOCK), BF16),
            pltpu.VMEM(w_out.shape, BF16),
            pltpu.VMEM((units, width), BF16),
            pltpu.VMEM((units, width), BF16),
            pltpu.VMEM(w_down.shape, BF16),
            pltpu.VMEM((2 * n * per, BLOCK), F32),
            pltpu.VMEM((2, CHUNKS, n, per, BLOCK), BF16),
            pltpu.VMEM((2, CHUNKS, nh, per, BLOCK), BF16),
            pltpu.VMEM((2, CHUNKS, nh, per, BLOCK), BF16),
            pltpu.VMEM((2, CHUNKS, nh, per, BLOCK), BF16),
            pltpu.VMEM((own * blocks, BLOCK), F32),
            pltpu.VMEM((own * blocks, BLOCK), F32),
            pltpu.VMEM((PARTS, n, piece, BLOCK), BF16),
            pltpu.VMEM((rows * blocks, BLOCK), F32),
            dma((CHUNKS + 6,)),
            dma((2, CHUNKS)), dma((2, CHUNKS)),
            dma((2, CHUNKS, nh)), dma((2, CHUNKS, nh)),
            dma((PARTS, nh)), dma((PARTS, nh)),
            dma((PARTS, nh)), dma((PARTS, nh)),
        ],
        compiler_params=pltpu.CompilerParams(
            collective_id=0, has_side_effects=True, vmem_limit_bytes=60 * 1024 * 1024
        ),
    )(residual, context, w_out, ffn_gain.reshape(blocks, BLOCK), w_gate.T, w_up.T, w_down)


def solution(mesh):
    return jax.shard_map(
        local,
        mesh=mesh,
        in_specs=(
            P(("groups", "tensor"), None),
            P("groups", "tensor"),
            P("tensor", None),
            P(),
            P(None, "tensor"),
            P(None, "tensor"),
            P("tensor", None),
        ),
        out_specs=P(("groups", "tensor"), None),
        check_vma=False,
    )
```
